1024 devices in a mesh: rows: 32 (over y_hi, z), cols: 32 (over y_lo, x, core).
Axes of the slice: x: 8, y: 8 (y_hi: 4, y_lo: 2; y = y_hi * 2 + y_lo), z: 8, core: 2. Of those that a mesh axis runs over, the one named last changes fastest.
Arguments:
- blocks: bfloat16 [512, 64, 128, 128], P('rows', 'cols'), may hold values from -0.5 to 0.5
- columns: int32 [512, 64], P('rows', 'cols'), may hold values from 0 to 511, as said below
- counts: int32 [512, 32], P('rows', 'cols'), may hold values from 1 to 2, as said below
- aggregate: int32 [512], replicated, may hold values from 0 to 63, as said below
- panels: bfloat16 [512, 24, 128], P('rows'), may hold values from -2.390625 to 2.390625
Outputs:
- coarse_band: float32 [64, 24, 1584], P('rows')
The draws below stay inside these ranges and needn't reach their ends.
Inputs may be any that keep to these rules, and one draw needn't show every extreme that they name: `columns`: the block column of a slot of block row i lies in the range of block rows (i // 16 + d) * 16 to (i // 16 + d + 1) * 16 - 1 for some d with |d| <= 16. Slots c * 2 to c * 2 + 1 of a block row form group c; slot c * 2 + j holds a block if and only if j < counts[i, c]. Some group has all 2 slots live. `aggregate`: the 16 block rows from r * 16 belong to aggregates r * 2 to r * 2 + 1, exactly 8 to each.
All inputs are finite; a program needn't handle non-finite values.
Results may differ from the reference program's by a relative error of at most 0.0029.
Values may be sent and summed in bfloat16 or wider, within the bound.
No kernel may reach another device: no remote copies, remote signals or barrier semaphores. Data moves between devices by JAX's collectives and lax.ppermute only.
A program may use at most 32 MiB of HBM per device.

```python
import jax
import jax.numpy as jnp
from jax import lax

BLK = 128
MODES = 24
BR_DEV = 16
KB_DEV = 2
SPAN = 16
NB = 512
KSLOT = 64
AGG_DEV = 2
NA = 64
WIN = 1584


def draw_columns(key, part):
    key = jax.random.fold_in(key, 11)
    first, second = jax.random.split(key, 2)
    devices = NB // BR_DEV
    home_device = jnp.arange(NB, dtype=jnp.int32) // BR_DEV
    offset = jax.random.randint(first, (NB, KSLOT), -SPAN, SPAN + 1, dtype=jnp.int32)
    target = jnp.clip(home_device[:, None] + offset, 0, devices - 1)
    within = jax.random.randint(second, (NB, KSLOT), 0, BR_DEV, dtype=jnp.int32)
    return (target * BR_DEV + within).astype(jnp.int32)


def draw_counts(key, part):
    key = jax.random.fold_in(key, 23)
    first, second, third = jax.random.split(key, 3)
    groups = KSLOT // KB_DEV
    values = jax.random.randint(first, (NB, groups), 1, KB_DEV + 1, dtype=jnp.int32)
    chosen_row = jax.random.randint(second, (), 0, NB, dtype=jnp.int32)
    chosen_group = jax.random.randint(third, (), 0, groups, dtype=jnp.int32)
    return values.at[chosen_row, chosen_group].set(KB_DEV).astype(jnp.int32)


def draw_aggregate(key, part):
    key = jax.random.fold_in(key, 37)
    devices = NB // BR_DEV
    device_keys = jax.random.split(key, devices)
    shuffled = jax.vmap(lambda one_key: jax.random.permutation(one_key, BR_DEV))(device_keys)
    home_device = jnp.arange(devices, dtype=jnp.int32)[:, None]
    return (home_device * AGG_DEV + shuffled.astype(jnp.int32) % AGG_DEV).reshape(NB).astype(jnp.int32)


def block_levels(key, shape, shards, least, largest):
    def one(dim, shards_of):
        draws = jax.random.uniform(jax.random.fold_in(jax.random.fold_in(key, 6), dim), (shards_of,), jnp.float32, least / len(shards), largest / len(shards))
        return jnp.repeat(jnp.exp(draws), shape[dim] // shards_of).reshape((-1,) + (1,) * (len(shape) - dim - 1))

    factor_of = one(*shards[0])
    for cut in shards[1:]:
        factor_of = factor_of * one(*cut)
    return factor_of


def normal_values(own_key, dims, width, most, pieces=(), held_as=jnp.bfloat16):
    drawn = width * jax.random.normal(own_key, dims, jnp.float32)
    if pieces:
        drawn = drawn * block_levels(own_key, dims, pieces, -0.22, 0.18)
    return jnp.clip(drawn, -most, most).astype(held_as)


def setup_inputs(seed: int = 0) -> dict:
    key_of = jax.random.split(jax.random.key(seed), 6)
    return {
        "blocks": normal_values(key_of[0], (NB, KSLOT, BLK, BLK), BLK ** -0.5, 0.5, ((0, 32), (1, 32))),
        "columns": draw_columns(jax.random.fold_in(key_of[5], 71), 0),
        "counts": draw_counts(jax.random.fold_in(key_of[5], 71), 0),
        "aggregate": draw_aggregate(jax.random.fold_in(key_of[5], 71), 0),
        "panels": normal_values(key_of[4], (NB, MODES, BLK), 0.3, 2.390625, ((0, 32),)),
    }


def reference(blocks, columns, counts, aggregate, panels):
    devices = NB // BR_DEV
    window_aggs = (2 * SPAN + 1) * AGG_DEV
    slot_range = jnp.arange(KSLOT, dtype=jnp.int32)
    slot_group = slot_range // KB_DEV
    slot_within = slot_range % KB_DEV

    def one_group(group):
        first_row = (group * BR_DEV).astype(jnp.int32)
        group_blocks = lax.dynamic_slice_in_dim(blocks, first_row, BR_DEV, 0)
        group_columns = lax.dynamic_slice_in_dim(columns, first_row, BR_DEV, 0)
        group_counts = lax.dynamic_slice_in_dim(counts, first_row, BR_DEV, 0)
        own_panels = lax.dynamic_slice_in_dim(panels, first_row, BR_DEV, 0)
        own_aggs = lax.dynamic_slice_in_dim(aggregate, first_row, BR_DEV, 0) - group * AGG_DEV
        slot_counts = jnp.take(group_counts, slot_group, axis=1)
        live_mask = (slot_within[None, :] < slot_counts).astype(jnp.float32)
        remote_panels = jnp.take(panels, group_columns.reshape(-1), axis=0).reshape(BR_DEV, KSLOT, MODES, BLK)
        product = jnp.einsum("iskl,isnl->isnk", group_blocks.astype(jnp.float32), remote_panels.astype(jnp.float32)).astype(jnp.bfloat16)
        triple = jnp.einsum("imk,isnk->ismn", own_panels.astype(jnp.float32), product.astype(jnp.float32))
        weighted = triple * live_mask[:, :, None, None]
        window_agg = jnp.take(aggregate, group_columns.reshape(-1), axis=0).reshape(BR_DEV, KSLOT) - (group - SPAN) * AGG_DEV
        column_hot = (window_agg[:, :, None] == jnp.arange(window_aggs, dtype=jnp.int32)[None, None, :]).astype(jnp.float32)
        row_hot = (own_aggs[:, None] == jnp.arange(AGG_DEV, dtype=jnp.int32)[None, :]).astype(jnp.float32)
        gathered = jnp.einsum("isb,ismn->imbn", column_hot, weighted, precision=lax.Precision.HIGHEST)
        coarse = jnp.einsum("ia,imbn->ambn", row_hot, gathered, precision=lax.Precision.HIGHEST)
        return coarse.reshape(AGG_DEV, MODES, window_aggs * MODES)

    result = lax.map(one_group, jnp.arange(devices, dtype=jnp.int32))
    return result.reshape(NA, MODES, WIN)
```

```python
import jax
import jax.numpy as jnp
import numpy as np
from jax import lax
from jax.experimental import pallas as pl
from jax.experimental.pallas import tpu as pltpu
from jax.sharding import Mesh
from jax.sharding import PartitionSpec as P

AXES = ("yh", "z", "yl", "xh", "xl", "k")
SIZES = (4, 8, 2, 4, 2, 2)
ROWS = ("yh", "z")
COLS = ("yl", "xh", "xl", "k")
SHARE = ("yl", "xl", "k")
QUAD = ("yl", "xl")

ROWS_HERE = 16
SLOTS = 32
MODES = 24
DOFS = 128
AGG_DEV = 2
PAIR = AGG_DEV * MODES
CODES = AGG_DEV * 4 * ROWS_HERE
PLANES = MODES + 1
WIN = 1584
LIMIT = 24 * 1024 * 1024


def left_kernel(blocks, columns, counts, aggregate, panels, out, wide):
    row = lax.axis_index("yh") * 8 + lax.axis_index("z")
    lane = lax.broadcasted_iota(jnp.int32, (1, DOFS), 1)
    for i in range(ROWS_HERE):
        both = jnp.concatenate([blocks[i, 0], blocks[i, 1]], axis=1)
        left = jnp.dot(panels[i], both, preferred_element_type=jnp.float32)
        count = counts[i, 0]
        own = aggregate[row * ROWS_HERE + i] - row * AGG_DEV
        for s in range(2):
            slot = 2 * i + s
            wide[pl.ds(slot, MODES, stride=SLOTS), :] = left[:, s * DOFS : (s + 1) * DOFS]
            column = columns[i, s]
            code = own * 64 + (column >> 7) * 16 + (column & 15)
            code = jnp.where(s < count, code, -1)
            depth = ((column >> 4) & 7).astype(jnp.float32)
            wide[pl.ds(MODES * SLOTS + slot, 1), :] = jnp.where(lane == code, depth, -1.0)
    total = wide[...].astype(jnp.bfloat16)
    for u in range(4):
        out[u] = total


def middle_kernel(near, far, panels, aggregate, out, wide):
    q = lax.axis_index("yl") * 4 + lax.axis_index("xl") * 2 + lax.axis_index("k")

    def plane(m):
        parts = [ref[u, m * SLOTS : (m + 1) * SLOTS, :] for ref in (near, far) for u in range(4)]
        return jnp.concatenate(parts, axis=0)

    codes = plane(MODES).astype(jnp.float32)
    hot = (jnp.transpose(codes) == q.astype(jnp.float32)).astype(jnp.float32).astype(jnp.bfloat16)
    for m in range(0, MODES, 2):
        pair = jnp.concatenate([plane(m), plane(m + 1)], axis=1)
        summed = jnp.dot(hot, pair, preferred_element_type=jnp.float32)
        wide[m * CODES : (m + 1) * CODES, :] = summed[:, :DOFS]
        wide[(m + 1) * CODES : (m + 2) * CODES, :] = summed[:, DOFS:]
    found = []
    for y in range(4):
        group = y * 8 + q
        lefts, rights = [], []
        for j in range(ROWS_HERE):
            a0 = wide[pl.ds(y * 16 + j, MODES, stride=CODES), :]
            a1 = wide[pl.ds(64 + y * 16 + j, MODES, stride=CODES), :]
            lefts.append(jnp.concatenate([a0, a1], axis=0))
            which = aggregate[group * ROWS_HERE + j] - group * AGG_DEV
            panel = panels[y, j].astype(jnp.float32)
            zero = jnp.zeros_like(panel)
            halves = [jnp.where(which == b, panel, zero) for b in range(AGG_DEV)]
            rights.append(jnp.concatenate(halves, axis=0).astype(jnp.bfloat16))
        left = jnp.concatenate(lefts, axis=1)
        high = left.astype(jnp.bfloat16)
        low = (left - high.astype(jnp.float32)).astype(jnp.bfloat16)
        right = jnp.concatenate(rights, axis=1)
        over = (((1,), (1,)), ((), ()))
        found.append(
            lax.dot_general(high, right, over, preferred_element_type=jnp.float32)
            + lax.dot_general(low, right, over, preferred_element_type=jnp.float32)
        )
    row = jnp.concatenate(found, axis=1)
    first = row[:, :128]
    rest = jnp.concatenate([row[:MODES, 128:], row[MODES:, 128:]], axis=1)
    for u in range(4):
        out[u, :PAIR, :] = first
        out[u, PAIR:, :] = rest


def place_kernel(parts, out, wide):
    row = lax.axis_index("yh") * 8 + lax.axis_index("z")
    lane = lax.broadcasted_iota(jnp.int32, (PAIR, 256), 1)
    windows = [jnp.zeros((PAIR, 256), jnp.float32) for _ in range(6)]
    for q in range(8):
        rest = parts[q, PAIR:, :]
        tail = jnp.concatenate([rest, pltpu.roll(rest, 64, axis=1)], axis=0)
        source = jnp.concatenate([parts[q, :PAIR, :], tail], axis=1)
        for y in range(4):
            start = (y * 8 + q) * PAIR
            at = start % 256
            turned = pltpu.roll(source, (start - y * PAIR) % 256, axis=1)
            w = start // 256
            windows[w] = jnp.where((lane >= at) & (lane < at + PAIR), turned, windows[w])
            if at + PAIR > 256:
                windows[w + 1] = jnp.where(lane < at + PAIR - 256, turned, windows[w + 1])
    wide[:, : 6 * 128] = jnp.zeros((PAIR, 6 * 128), jnp.float32)
    wide[:, 18 * 128 :] = jnp.zeros((PAIR, 7 * 128), jnp.float32)
    for w in range(6):
        wide[:, (6 + 2 * w) * 128 : (8 + 2 * w) * 128] = windows[w]
    offset = row * PAIR
    base = pl.multiple_of((offset // 128) * 128, 128)
    shift = offset % 128
    narrow = lax.broadcasted_iota(jnp.int32, (PAIR, 128), 1)
    turned = []
    for t in range(14):
        tile = wide[:, pl.ds(base + t * 128, 128)]
        turned.append(pltpu.roll(tile, (128 - shift) % 128, axis=1))
    for t in range(13):
        tile = jnp.where(narrow < 128 - shift, turned[t], turned[t + 1])
        width = min(128, WIN - t * 128)
        for a in range(AGG_DEV):
            out[a, :, t * 128 : t * 128 + width] = tile[a * MODES : (a + 1) * MODES, :width]


def everything(space, count):
    return [pl.BlockSpec(memory_space=space) for _ in range(count)]


VMEM, SMEM = pltpu.VMEM, pltpu.SMEM


def local(blocks, columns, counts, aggregate, panels):
    f32, bf16 = jnp.float32, jnp.bfloat16
    params = pltpu.CompilerParams(vmem_limit_bytes=LIMIT)

    pairs = []
    for yh, z, yl, xh, xl, k in np.ndindex(*SIZES):
        source = (yh, yl * 4 + xl * 2 + k, (z >> 2) & 1, xh, (z >> 1) & 1, z & 1)
        pairs.append(
            (int(np.ravel_multi_index(source, SIZES)), int(np.ravel_multi_index((yh, z, yl, xh, xl, k), SIZES)))
        )
    turned = lax.ppermute(panels, AXES, pairs)
    gathered = lax.all_to_all(
        jnp.broadcast_to(turned[None], (4,) + turned.shape), "yh", 0, 0, tiled=True
    )

    left = pl.pallas_call(
        left_kernel,
        out_shape=jax.ShapeDtypeStruct((4, PLANES * SLOTS, DOFS), bf16),
        in_specs=[
            pl.BlockSpec(memory_space=VMEM),
            pl.BlockSpec(memory_space=SMEM),
            pl.BlockSpec(memory_space=SMEM),
            pl.BlockSpec(memory_space=SMEM),
            pl.BlockSpec(memory_space=VMEM),
        ],
        out_specs=pl.BlockSpec(memory_space=VMEM),
        scratch_shapes=[pltpu.VMEM((PLANES * SLOTS, DOFS), f32)],
        compiler_params=params,
        cost_estimate=pl.CostEstimate(flops=25_000_000, bytes_accessed=2_000_000, transcendentals=0),
        name="left",
    )(blocks, columns, counts, aggregate, panels)
    near = lax.all_to_all(left, QUAD, 0, 0, tiled=True)
    far = lax.ppermute(near, "k", [(0, 1), (1, 0)])

    part = pl.pallas_call(
        middle_kernel,
        out_shape=jax.ShapeDtypeStruct((4, PAIR + MODES, DOFS), f32),
        in_specs=[
            pl.BlockSpec(memory_space=VMEM),
            pl.BlockSpec(memory_space=VMEM),
            pl.BlockSpec(memory_space=VMEM),
            pl.BlockSpec(memory_space=SMEM),
        ],
        out_specs=pl.BlockSpec(memory_space=VMEM),
        scratch_shapes=[pltpu.VMEM((MODES * CODES, DOFS), f32)],
        compiler_params=params,
        cost_estimate=pl.CostEstimate(flops=500_000_000, bytes_accessed=3_000_000, transcendentals=0),
        name="middle",
    )(near, far, gathered, aggregate)

    shares = lax.all_to_all(part, "xh", 0, 0, tiled=True)
    whole = jnp.sum(shares, axis=0)
    spread = lax.all_to_all(
        jnp.broadcast_to(whole[None], (8,) + whole.shape), SHARE, 0, 0, tiled=True
    )
    return pl.pallas_call(
        place_kernel,
        out_shape=jax.ShapeDtypeStruct((AGG_DEV, MODES, WIN), f32),
        in_specs=[pl.BlockSpec(memory_space=VMEM)],
        out_specs=pl.BlockSpec(memory_space=VMEM),
        scratch_shapes=[pltpu.VMEM((PAIR, 25 * 128), f32)],
        compiler_params=params,
        cost_estimate=pl.CostEstimate(flops=1_000_000, bytes_accessed=600_000, transcendentals=0),
        name="place",
    )(spread)


def solution(mesh):
    inner = Mesh(mesh.devices.reshape(SIZES), AXES)
    return jax.shard_map(
        local,
        mesh=inner,
        in_specs=(
            P(ROWS, COLS, None, None),
            P(ROWS, COLS),
            P(ROWS, COLS),
            P(),
            P(ROWS, None, None),
        ),
        out_specs=P(ROWS, None, None),
        check_vma=False,
    )
```

```python
import jax
import jax.numpy as jnp
import numpy as np
from jax import lax
from jax.experimental import pallas as pl
from jax.experimental.pallas import tpu as pltpu
from jax.sharding import Mesh
from jax.sharding import PartitionSpec as P

AXES = ("yh", "zh", "zl", "yl", "xh", "xl", "k")
SIZES = (4, 4, 2, 2, 4, 2, 2)
ROWS = ("yh", "zh", "zl")
COLS = ("yl", "xh", "xl", "k")
SHARE = ("yl", "xl", "k")
QUAD = ("yl", "xl")

ROWS_HERE = 16
SLOTS = 32
MODES = 24
DOFS = 128
AGG_DEV = 2
PAIR = AGG_DEV * MODES
CODES = AGG_DEV * 4 * ROWS_HERE
PLANES = MODES + 1
WIN = 1584
LIMIT = 24 * 1024 * 1024
FULL = 63 * 1024 * 1024


def left_kernel(*refs):
    far = refs[:5]
    out, wide, blocks, columns, counts, aggregate, panels, arrived = refs[5:]
    pieces = 4
    step = ROWS_HERE // pieces
    copies = [
        pltpu.make_async_copy(far[n], here, arrived.at[n])
        for n, here in ((1, columns), (2, counts), (3, aggregate), (4, panels))
    ]
    for p in range(pieces):
        part = pl.ds(p * step, step)
        copies.append(pltpu.make_async_copy(far[0].at[part], blocks.at[part], arrived.at[5 + p]))
    for copy in copies:
        copy.start()
    for copy in copies[:3]:
        copy.wait()
    row = lax.axis_index("yh") * 8 + lax.axis_index("zh") * 2 + lax.axis_index("zl")
    lane = lax.broadcasted_iota(jnp.int32, (1, DOFS), 1)
    for i in range(ROWS_HERE):
        count = counts[0, i]
        own = aggregate[row * ROWS_HERE + i] - row * AGG_DEV
        for s in range(2):
            column = columns[s, i]
            code = own * 64 + ((column >> 5) & 3) * 16 + (column & 15)
            code = jnp.where(s < count, code, -1)
            place = ((column >> 7) * 2 + ((column >> 4) & 1)).astype(jnp.float32)
            at = MODES * SLOTS + 2 * i + s
            wide[pl.ds(at, 1), :] = jnp.where(lane == code, place, -1.0)
    copies[3].wait()
    for i in range(ROWS_HERE):
        if i % step == 0:
            copies[4 + i // step].wait()
        both = jnp.concatenate([blocks[i, 0], blocks[i, 1]], axis=1)
        left = jnp.dot(panels[i], both, preferred_element_type=jnp.float32)
        for s in range(2):
            wide[pl.ds(2 * i + s, MODES, stride=SLOTS), :] = left[:, s * DOFS : (s + 1) * DOFS]
    out[...] = wide[...].astype(jnp.bfloat16)


def middle_kernel(near, far, panels, aggregate_far, out, wide, aggregate, arrived):
    copy = pltpu.make_async_copy(aggregate_far, aggregate, arrived)
    copy.start()
    q = lax.axis_index("yl") * 4 + lax.axis_index("xl") * 2 + lax.axis_index("k")

    def plane(m):
        parts = [ref[u, m * SLOTS : (m + 1) * SLOTS, :] for ref in (near, far) for u in range(4)]
        return jnp.concatenate(parts, axis=0)

    codes = plane(MODES).astype(jnp.float32)
    hot = (jnp.transpose(codes) == q.astype(jnp.float32)).astype(jnp.float32).astype(jnp.bfloat16)
    for m in range(0, MODES, 2):
        pair = jnp.concatenate([plane(m), plane(m + 1)], axis=1)
        summed = jnp.dot(hot, pair, preferred_element_type=jnp.float32)
        wide[m * CODES : (m + 1) * CODES, :] = summed[:, :DOFS]
        wide[(m + 1) * CODES : (m + 2) * CODES, :] = summed[:, DOFS:]
    copy.wait()
    found = []
    for y in range(4):
        group = (q >> 1) * 8 + y * 2 + (q & 1)
        lefts, rights = [], []
        for j in range(ROWS_HERE):
            a0 = wide[pl.ds(y * 16 + j, MODES, stride=CODES), :]
            a1 = wide[pl.ds(64 + y * 16 + j, MODES, stride=CODES), :]
            lefts.append(jnp.concatenate([a0, a1], axis=0))
            which = aggregate[group * ROWS_HERE + j] - group * AGG_DEV
            panel = panels[y, j].astype(jnp.float32)
            zero = jnp.zeros_like(panel)
            halves = [jnp.where(which == b, panel, zero) for b in range(AGG_DEV)]
            rights.append(jnp.concatenate(halves, axis=0).astype(jnp.bfloat16))
        left = jnp.concatenate(lefts, axis=1)
        high = left.astype(jnp.bfloat16)
        low = (left - high.astype(jnp.float32)).astype(jnp.bfloat16)
        right = jnp.concatenate(rights, axis=1)
        over = (((1,), (1,)), ((), ()))
        found.append(
            lax.dot_general(high, right, over, preferred_element_type=jnp.float32)
            + lax.dot_general(low, right, over, preferred_element_type=jnp.float32)
        )
    row = jnp.concatenate(found, axis=1)
    first = row[:, :128]
    rest = jnp.concatenate([row[:MODES, 128:], row[MODES:, 128:]], axis=1)
    for u in range(4):
        out[u, :PAIR, :] = first
        out[u, PAIR:, :] = rest


def place_kernel(parts, out, wide):
    row = lax.axis_index("yh") * 8 + lax.axis_index("zh") * 2 + lax.axis_index("zl")
    lane = lax.broadcasted_iota(jnp.int32, (PAIR, 256), 1)
    windows = [jnp.zeros((PAIR, 256), jnp.float32) for _ in range(6)]
    for q in range(8):
        rest = parts[q, PAIR:, :]
        tail = jnp.concatenate([rest, pltpu.roll(rest, 64, axis=1)], axis=0)
        source = jnp.concatenate([parts[q, :PAIR, :], tail], axis=1)
        for y in range(4):
            start = ((q >> 1) * 8 + y * 2 + (q & 1)) * PAIR
            at = start % 256
            turned = pltpu.roll(source, (start - y * PAIR) % 256, axis=1)
            w = start // 256
            windows[w] = jnp.where((lane >= at) & (lane < at + PAIR), turned, windows[w])
            if at + PAIR > 256:
                windows[w + 1] = jnp.where(lane < at + PAIR - 256, turned, windows[w + 1])
    wide[:, : 6 * 128] = jnp.zeros((PAIR, 6 * 128), jnp.float32)
    wide[:, 18 * 128 :] = jnp.zeros((PAIR, 7 * 128), jnp.float32)
    for w in range(6):
        wide[:, (6 + 2 * w) * 128 : (8 + 2 * w) * 128] = windows[w]
    offset = row * PAIR
    base = pl.multiple_of((offset // 128) * 128, 128)
    shift = offset % 128
    narrow = lax.broadcasted_iota(jnp.int32, (PAIR, 128), 1)
    turned = []
    for t in range(14):
        tile = wide[:, pl.ds(base + t * 128, 128)]
        turned.append(pltpu.roll(tile, (128 - shift) % 128, axis=1))
    for t in range(13):
        tile = jnp.where(narrow < 128 - shift, turned[t], turned[t + 1])
        width = min(128, WIN - t * 128)
        for a in range(AGG_DEV):
            out[a, :, t * 128 : t * 128 + width] = tile[a * MODES : (a + 1) * MODES, :width]


def everything(space, count):
    return [pl.BlockSpec(memory_space=space) for _ in range(count)]


VMEM, SMEM = pltpu.VMEM, pltpu.SMEM


def local(blocks, columns, counts, aggregate, panels):
    f32, bf16 = jnp.float32, jnp.bfloat16
    params = pltpu.CompilerParams(vmem_limit_bytes=LIMIT)

    pairs = []
    for yh, zh, zl, yl, xh, xl, k in np.ndindex(*SIZES):
        source = (yl * 2 + xl, zh, k, yh >> 1, xh, yh & 1, zl)
        target = (yh, zh, zl, yl, xh, xl, k)
        pairs.append(tuple(int(np.ravel_multi_index(at, SIZES)) for at in (source, target)))
    turned = lax.ppermute(panels, AXES, pairs)

    left = pl.pallas_call(
        left_kernel,
        out_shape=jax.ShapeDtypeStruct((PLANES * SLOTS, DOFS), bf16),
        in_specs=everything(pltpu.HBM, 5),
        out_specs=pl.BlockSpec(memory_space=VMEM),
        scratch_shapes=[
            pltpu.VMEM((PLANES * SLOTS, DOFS), f32),
            pltpu.VMEM(blocks.shape, bf16),
            pltpu.SMEM((2, ROWS_HERE), jnp.int32),
            pltpu.SMEM((1, ROWS_HERE), jnp.int32),
            pltpu.SMEM(aggregate.shape, jnp.int32),
            pltpu.VMEM(panels.shape, bf16),
            pltpu.SemaphoreType.DMA((9,)),
        ],
        compiler_params=pltpu.CompilerParams(vmem_limit_bytes=FULL),
        cost_estimate=pl.CostEstimate(flops=25_000_000, bytes_accessed=2_000_000, transcendentals=0),
        name="left",
    )(blocks, columns.T, counts.T, aggregate, panels)
    left, turned = lax.optimization_barrier((left, turned))
    swap = [(0, 1), (1, 0)]
    cross = [(0, 3), (1, 2), (2, 1), (3, 0)]
    beside = lax.ppermute(left, "xl", swap)
    above = lax.ppermute(left, "yl", swap)
    across = lax.ppermute(left, QUAD, cross)
    gathered = lax.all_to_all(
        jnp.broadcast_to(turned[None], (4,) + turned.shape), "zh", 0, 0, tiled=True
    )
    beside, above, across, gathered = lax.optimization_barrier((beside, above, across, gathered))
    near = jnp.stack([left, beside, above, across])
    far = lax.ppermute(near, "k", swap)

    part = pl.pallas_call(
        middle_kernel,
        out_shape=jax.ShapeDtypeStruct((4, PAIR + MODES, DOFS), f32),
        in_specs=[
            pl.BlockSpec(memory_space=VMEM),
            pl.BlockSpec(memory_space=VMEM),
            pl.BlockSpec(memory_space=VMEM),
            pl.BlockSpec(memory_space=pltpu.HBM),
        ],
        out_specs=pl.BlockSpec(memory_space=VMEM),
        scratch_shapes=[
            pltpu.VMEM((MODES * CODES, DOFS), f32),
            pltpu.SMEM(aggregate.shape, jnp.int32),
            pltpu.SemaphoreType.DMA,
        ],
        compiler_params=params,
        cost_estimate=pl.CostEstimate(flops=500_000_000, bytes_accessed=3_000_000, transcendentals=0),
        name="middle",
    )(near, far, gathered, aggregate)

    shares = lax.all_to_all(part, "xh", 0, 0, tiled=True)
    whole = jnp.sum(shares, axis=0)
    spread = lax.all_to_all(
        jnp.broadcast_to(whole[None], (8,) + whole.shape), SHARE, 0, 0, tiled=True
    )
    return pl.pallas_call(
        place_kernel,
        out_shape=jax.ShapeDtypeStruct((AGG_DEV, MODES, WIN), f32),
        in_specs=[pl.BlockSpec(memory_space=VMEM)],
        out_specs=pl.BlockSpec(memory_space=VMEM),
        scratch_shapes=[pltpu.VMEM((PAIR, 25 * 128), f32)],
        compiler_params=params,
        cost_estimate=pl.CostEstimate(flops=1_000_000, bytes_accessed=600_000, transcendentals=0),
        name="place",
    )(spread)


def solution(mesh):
    inner = Mesh(mesh.devices.reshape(SIZES), AXES)
    return jax.shard_map(
        local,
        mesh=inner,
        in_specs=(
            P(ROWS, COLS, None, None),
            P(ROWS, COLS),
            P(ROWS, COLS),
            P(),
            P(ROWS, None, None),
        ),
        out_specs=P(ROWS, None, None),
        check_vma=False,
    )
```

```python
import functools

import jax
import jax.numpy as jnp
import numpy as np
from jax import lax
from jax.experimental import pallas as pl
from jax.experimental.pallas import tpu as pltpu
from jax.sharding import Mesh
from jax.sharding import PartitionSpec as P

AXES = ("yh", "zh", "zl", "yl", "xh", "xl", "k")
SIZES = (4, 4, 2, 2, 4, 2, 2)
ROWS = ("yh", "zh", "zl")
COLS = ("yl", "xh", "xl", "k")
SHARE = ("yl", "xl", "k")
QUAD = ("yl", "xl")

ROWS_HERE = 16
SLOTS = 32
MODES = 24
DOFS = 128
AGG_DEV = 2
PAIR = AGG_DEV * MODES
CODES = AGG_DEV * 4 * ROWS_HERE
EARLY = 2
PLANES = MODES + 1
WIN = 1584
LIMIT = 24 * 1024 * 1024
FULL = 63 * 1024 * 1024


def left_kernel(*refs):
    far = refs[:5]
    out, wide, blocks, columns, counts, aggregate, panels, arrived = refs[5:]
    pieces = 4
    step = ROWS_HERE // pieces
    copies = [
        pltpu.make_async_copy(far[n], here, arrived.at[n])
        for n, here in ((1, columns), (2, counts), (3, aggregate), (4, panels))
    ]
    for p in range(pieces):
        part = pl.ds(p * step, step)
        copies.append(pltpu.make_async_copy(far[0].at[part], blocks.at[part], arrived.at[5 + p]))
    for copy in copies:
        copy.start()
    for copy in copies[:3]:
        copy.wait()
    row = lax.axis_index("yh") * 8 + lax.axis_index("zh") * 2 + lax.axis_index("zl")
    lane = lax.broadcasted_iota(jnp.int32, (1, DOFS), 1)
    for i in range(ROWS_HERE):
        count = counts[0, i]
        own = aggregate[row * ROWS_HERE + i] - row * AGG_DEV
        for s in range(2):
            column = columns[s, i]
            code = own * 64 + ((column >> 5) & 3) * 16 + (column & 15)
            code = jnp.where(s < count, code, -1)
            place = ((column >> 7) * 2 + ((column >> 4) & 1)).astype(jnp.float32)
            at = MODES * SLOTS + 2 * i + s
            wide[pl.ds(at, 1), :] = jnp.where(lane == code, place, -1.0)
    copies[3].wait()
    for i in range(ROWS_HERE):
        if i % step == 0:
            copies[4 + i // step].wait()
        both = jnp.concatenate([blocks[i, 0], blocks[i, 1]], axis=1)
        left = jnp.dot(panels[i], both, preferred_element_type=jnp.float32)
        for s in range(2):
            wide[pl.ds(2 * i + s, MODES, stride=SLOTS), :] = left[:, s * DOFS : (s + 1) * DOFS]
    out[...] = wide[...].astype(jnp.bfloat16)


def spread_kernel(one, out, arrived):
    copies = [pltpu.make_async_copy(one, out.at[u], arrived.at[u]) for u in range(4)]
    for copy in copies:
        copy.start()
    for copy in copies:
        copy.wait()


def halves_kernel(aggregate_far, out, aggregate, arrived):
    copy = pltpu.make_async_copy(aggregate_far, aggregate, arrived)
    copy.start()
    copy.wait()
    q = lax.axis_index("yl") * 4 + lax.axis_index("xl") * 2 + lax.axis_index("k")
    for y in range(4):
        group = (q >> 1) * 8 + y * 2 + (q & 1)
        for j in range(ROWS_HERE):
            which = aggregate[group * ROWS_HERE + j] - group * AGG_DEV
            out[pl.ds(y * ROWS_HERE + j, 1), :] = jnp.full((1, DOFS), which, jnp.int32).astype(jnp.float32)


def middle_kernel(near, far, far_late, panels, which, out, wide):
    q = lax.axis_index("yl") * 4 + lax.axis_index("xl") * 2 + lax.axis_index("k")

    def plane(m):
        rows = slice(m * SLOTS, (m + 1) * SLOTS)
        parts = [near[u, rows, :] for u in range(4)] + [far[u, rows, :] + far_late[u, rows, :] for u in range(4)]
        return jnp.concatenate(parts, axis=0)

    codes = plane(MODES).astype(jnp.float32)
    hot = (jnp.transpose(codes) == q.astype(jnp.float32)).astype(jnp.float32).astype(jnp.bfloat16)
    for m in range(0, MODES, 2):
        pair = jnp.concatenate([plane(m), plane(m + 1)], axis=1)
        summed = jnp.dot(hot, pair, preferred_element_type=jnp.float32)
        wide[m * CODES : (m + 1) * CODES, :] = summed[:, :DOFS]
        wide[(m + 1) * CODES : (m + 2) * CODES, :] = summed[:, DOFS:]
    found = []
    for y in range(4):
        lefts, rights = [], []
        for j in range(ROWS_HERE):
            a0 = wide[pl.ds(y * 16 + j, MODES, stride=CODES), :]
            a1 = wide[pl.ds(64 + y * 16 + j, MODES, stride=CODES), :]
            lefts.append(jnp.concatenate([a0, a1], axis=0))
            side = jnp.broadcast_to(which[pl.ds(y * ROWS_HERE + j, 1), :], (MODES, DOFS))
            panel = panels[y, j].astype(jnp.float32)
            zero = jnp.zeros_like(panel)
            halves = [jnp.where(side == float(b), panel, zero) for b in range(AGG_DEV)]
            rights.append(jnp.concatenate(halves, axis=0).astype(jnp.bfloat16))
        left = jnp.concatenate(lefts, axis=1)
        high = left.astype(jnp.bfloat16)
        low = (left - high.astype(jnp.float32)).astype(jnp.bfloat16)
        right = jnp.concatenate(rights, axis=1)
        over = (((1,), (1,)), ((), ()))
        found.append(
            lax.dot_general(high, right, over, preferred_element_type=jnp.float32)
            + lax.dot_general(low, right, over, preferred_element_type=jnp.float32)
        )
    row = jnp.concatenate(found, axis=1)
    first = row[:, :128]
    rest = jnp.concatenate([row[:MODES, 128:], row[MODES:, 128:]], axis=1)
    for u in range(4):
        out[u, :PAIR, :] = first
        out[u, PAIR:, :] = rest


def place_kernel(parts, out, wide):
    row = lax.axis_index("yh") * 8 + lax.axis_index("zh") * 2 + lax.axis_index("zl")
    lane = lax.broadcasted_iota(jnp.int32, (PAIR, 256), 1)
    windows = [jnp.zeros((PAIR, 256), jnp.float32) for _ in range(6)]
    for q in range(8):
        rest = parts[q, PAIR:, :]
        tail = jnp.concatenate([rest, pltpu.roll(rest, 64, axis=1)], axis=0)
        source = jnp.concatenate([parts[q, :PAIR, :], tail], axis=1)
        for y in range(4):
            start = ((q >> 1) * 8 + y * 2 + (q & 1)) * PAIR
            at = start % 256
            turned = pltpu.roll(source, (start - y * PAIR) % 256, axis=1)
            w = start // 256
            windows[w] = jnp.where((lane >= at) & (lane < at + PAIR), turned, windows[w])
            if at + PAIR > 256:
                windows[w + 1] = jnp.where(lane < at + PAIR - 256, turned, windows[w + 1])
    wide[:, : 6 * 128] = jnp.zeros((PAIR, 6 * 128), jnp.float32)
    wide[:, 18 * 128 :] = jnp.zeros((PAIR, 7 * 128), jnp.float32)
    for w in range(6):
        wide[:, (6 + 2 * w) * 128 : (8 + 2 * w) * 128] = windows[w]
    offset = row * PAIR
    base = pl.multiple_of((offset // 128) * 128, 128)
    shift = offset % 128
    narrow = lax.broadcasted_iota(jnp.int32, (PAIR, 128), 1)
    turned = []
    for t in range(14):
        tile = wide[:, pl.ds(base + t * 128, 128)]
        turned.append(pltpu.roll(tile, (128 - shift) % 128, axis=1))
    for t in range(13):
        tile = jnp.where(narrow < 128 - shift, turned[t], turned[t + 1])
        width = min(128, WIN - t * 128)
        for a in range(AGG_DEV):
            out[a, :, t * 128 : t * 128 + width] = tile[a * MODES : (a + 1) * MODES, :width]


def everything(space, count):
    return [pl.BlockSpec(memory_space=space) for _ in range(count)]


VMEM, SMEM = pltpu.VMEM, pltpu.SMEM


def local(blocks, columns, counts, aggregate, panels):
    f32, bf16 = jnp.float32, jnp.bfloat16
    params = pltpu.CompilerParams(vmem_limit_bytes=LIMIT)

    pairs = []
    for yh, zh, zl, yl, xh, xl, k in np.ndindex(*SIZES):
        source = (yl * 2 + xl, zh, k, yh >> 1, xh, yh & 1, zl)
        target = (yh, zh, zl, yl, xh, xl, k)
        pairs.append(tuple(int(np.ravel_multi_index(at, SIZES)) for at in (source, target)))
    turned = lax.ppermute(panels, AXES, pairs)

    left = pl.pallas_call(
        left_kernel,
        out_shape=jax.ShapeDtypeStruct((PLANES * SLOTS, DOFS), bf16),
        in_specs=everything(pltpu.HBM, 5),
        out_specs=pl.BlockSpec(memory_space=VMEM),
        scratch_shapes=[
            pltpu.VMEM((PLANES * SLOTS, DOFS), f32),
            pltpu.VMEM(blocks.shape, bf16),
            pltpu.SMEM((2, ROWS_HERE), jnp.int32),
            pltpu.SMEM((1, ROWS_HERE), jnp.int32),
            pltpu.SMEM(aggregate.shape, jnp.int32),
            pltpu.VMEM(panels.shape, bf16),
            pltpu.SemaphoreType.DMA((9,)),
        ],
        compiler_params=pltpu.CompilerParams(vmem_limit_bytes=FULL),
        cost_estimate=pl.CostEstimate(flops=25_000_000, bytes_accessed=2_000_000, transcendentals=0),
        name="left",
    )(blocks, columns.T, counts.T, aggregate, panels)
    def flips(early, *names):
        pairs = []
        for at in np.ndindex(*SIZES):
            if (at[1] < EARLY) == early:
                to = tuple(1 - c if n in names else c for n, c in zip(AXES, at))
                pairs.append((int(np.ravel_multi_index(at, SIZES)), int(np.ravel_multi_index(to, SIZES))))
        return pairs

    def around(x, early):
        return [lax.ppermute(x, AXES, flips(early, *names)) for names in (("xl",), ("yl",), ("yl", "xl"))]

    which = pl.pallas_call(
        halves_kernel,
        out_shape=jax.ShapeDtypeStruct((4 * ROWS_HERE, DOFS), f32),
        in_specs=everything(pltpu.HBM, 1),
        out_specs=pl.BlockSpec(memory_space=VMEM),
        scratch_shapes=[pltpu.SMEM(aggregate.shape, jnp.int32), pltpu.SemaphoreType.DMA],
        compiler_params=params,
        cost_estimate=pl.CostEstimate(flops=100_000_000_000, bytes_accessed=1_000, transcendentals=0),
        name="halves",
    )(aggregate)
    early = around(left, True)
    far_early = lax.ppermute(jnp.stack([left, *early]), AXES, flips(True, "k"))
    copies = pl.pallas_call(
        spread_kernel,
        out_shape=jax.ShapeDtypeStruct((4,) + turned.shape, bf16),
        in_specs=[pl.BlockSpec(memory_space=VMEM)],
        out_specs=pl.BlockSpec(memory_space=pl.ANY),
        scratch_shapes=[pltpu.SemaphoreType.DMA((4,))],
        compiler_params=params,
        cost_estimate=pl.CostEstimate(flops=100_000_000_000, bytes_accessed=500_000, transcendentals=0),
        name="copies",
    )(turned)
    gathered = lax.all_to_all(copies, "zh", 0, 0, tiled=True)
    left_later, far_early, which = lax.optimization_barrier((left, far_early, which))
    late = around(left_later, False)
    late, gathered = lax.optimization_barrier((late, gathered))
    near = jnp.stack([left, *(one + two for one, two in zip(early, late))])
    far_late = lax.ppermute(near, AXES, flips(False, "k"))

    part = pl.pallas_call(
        middle_kernel,
        out_shape=jax.ShapeDtypeStruct((4, PAIR + MODES, DOFS), f32),
        in_specs=[
            pl.BlockSpec(memory_space=VMEM),
            pl.BlockSpec(memory_space=VMEM),
            pl.BlockSpec(memory_space=VMEM),
            pl.BlockSpec(memory_space=VMEM),
            pl.BlockSpec(memory_space=VMEM),
        ],
        out_specs=pl.BlockSpec(memory_space=VMEM),
        scratch_shapes=[pltpu.VMEM((MODES * CODES, DOFS), f32)],
        compiler_params=params,
        cost_estimate=pl.CostEstimate(flops=500_000_000, bytes_accessed=3_000_000, transcendentals=0),
        name="middle",
    )(near, far_early, far_late, gathered, which)

    shares = lax.all_to_all(part, "xh", 0, 0, tiled=True)
    whole = jnp.sum(shares, axis=0)
    spread = lax.all_to_all(
        jnp.broadcast_to(whole[None], (8,) + whole.shape), SHARE, 0, 0, tiled=True
    )
    return pl.pallas_call(
        place_kernel,
        out_shape=jax.ShapeDtypeStruct((AGG_DEV, MODES, WIN), f32),
        in_specs=[pl.BlockSpec(memory_space=VMEM)],
        out_specs=pl.BlockSpec(memory_space=VMEM),
        scratch_shapes=[pltpu.VMEM((PAIR, 25 * 128), f32)],
        compiler_params=params,
        cost_estimate=pl.CostEstimate(flops=1_000_000, bytes_accessed=600_000, transcendentals=0),
        name="place",
    )(spread)


def solution(mesh):
    inner = Mesh(mesh.devices.reshape(SIZES), AXES)
    return jax.shard_map(
        local,
        mesh=inner,
        in_specs=(
            P(ROWS, COLS, None, None),
            P(ROWS, COLS),
            P(ROWS, COLS),
            P(),
            P(ROWS, None, None),
        ),
        out_specs=P(ROWS, None, None),
        check_vma=False,
    )
```

```python
import functools

import jax
import jax.numpy as jnp
import numpy as np
from jax import lax
from jax.experimental import pallas as pl
from jax.experimental.pallas import tpu as pltpu
from jax.sharding import Mesh
from jax.sharding import PartitionSpec as P

AXES = ("yh", "zh", "zl", "yl", "xh", "xl", "k")
SIZES = (4, 4, 2, 2, 4, 2, 2)
ROWS = ("yh", "zh", "zl")
COLS = ("yl", "xh", "xl", "k")
SHARE = ("yl", "xl", "k")
QUAD = ("yl", "xl")

ROWS_HERE = 16
SLOTS = 32
MODES = 24
DOFS = 128
AGG_DEV = 2
PAIR = AGG_DEV * MODES
CODES = AGG_DEV * 4 * ROWS_HERE
EARLY = 2
PLANES = MODES + 1
WIN = 1584
LIMIT = 24 * 1024 * 1024
FULL = 63 * 1024 * 1024


def member(yh, ahead):
    odd = ahead & 1
    return odd * (4 - ahead) + (1 - odd) * 2 * ((ahead >> 1) ^ (yh >> 1))


def ahead_of(yh, yl, xl):
    return xl * (3 - 2 * yl) + (1 - xl) * 2 * (yl ^ (yh >> 1))


def left_kernel(*refs):
    far = refs[:5]
    out, wide, blocks, columns, counts, aggregate, panels, arrived = refs[5:]
    pieces = 4
    step = ROWS_HERE // pieces
    copies = [
        pltpu.make_async_copy(far[n], here, arrived.at[n])
        for n, here in ((1, columns), (2, counts), (3, aggregate), (4, panels))
    ]
    for p in range(pieces):
        part = pl.ds(p * step, step)
        copies.append(pltpu.make_async_copy(far[0].at[part], blocks.at[part], arrived.at[5 + p]))
    for copy in copies:
        copy.start()
    for copy in copies[:3]:
        copy.wait()
    row = lax.axis_index("yh") * 8 + lax.axis_index("zh") * 2 + lax.axis_index("zl")
    yh, zl = lax.axis_index("yh"), lax.axis_index("zl")
    lane = lax.broadcasted_iota(jnp.int32, (1, DOFS), 1)
    for i in range(ROWS_HERE):
        count = counts[0, i]
        own = aggregate[row * ROWS_HERE + i] - row * AGG_DEV
        for s in range(2):
            column = columns[s, i]
            code = own * 64 + ((column >> 5) & 3) * 16 + (column & 15)
            code = jnp.where(s < count, code, -1)
            place = member(yh, ((column >> 7) - yh) & 3) * 2 + (((column >> 4) & 1) ^ zl)
            at = MODES * SLOTS + 2 * i + s
            wide[pl.ds(at, 1), :] = jnp.where(lane == code, place, -1).astype(jnp.float32)
    copies[3].wait()
    for i in range(ROWS_HERE):
        if i % step == 0:
            copies[4 + i // step].wait()
        both = jnp.concatenate([blocks[i, 0], blocks[i, 1]], axis=1)
        left = jnp.dot(panels[i], both, preferred_element_type=jnp.float32)
        for s in range(2):
            wide[pl.ds(2 * i + s, MODES, stride=SLOTS), :] = left[:, s * DOFS : (s + 1) * DOFS]
    out[...] = wide[...].astype(jnp.bfloat16)


def spread_kernel(one, out, arrived):
    copies = [pltpu.make_async_copy(one, out.at[u], arrived.at[u]) for u in range(4)]
    for copy in copies:
        copy.start()
    for copy in copies:
        copy.wait()


def halves_kernel(aggregate_far, out, aggregate, arrived):
    copy = pltpu.make_async_copy(aggregate_far, aggregate, arrived)
    copy.start()
    copy.wait()
    yh = lax.axis_index("yh")
    high = (yh + ahead_of(yh, lax.axis_index("yl"), lax.axis_index("xl"))) & 3
    low = lax.axis_index("zl") ^ lax.axis_index("k")
    for y in range(4):
        group = high * 8 + y * 2 + low
        for j in range(ROWS_HERE):
            which = aggregate[group * ROWS_HERE + j] - group * AGG_DEV
            out[pl.ds(y * ROWS_HERE + j, 1), :] = jnp.full((1, DOFS), which, jnp.int32).astype(jnp.float32)


def middle_kernel(near, far, far_late, panels, which, out, wide):
    q = lax.axis_index("yl") * 4 + lax.axis_index("xl") * 2 + lax.axis_index("k")

    def plane(m):
        rows = slice(m * SLOTS, (m + 1) * SLOTS)
        parts = [near[u, rows, :] for u in range(4)] + [far[u, rows, :] + far_late[u, rows, :] for u in range(4)]
        return jnp.concatenate(parts, axis=0)

    codes = plane(MODES).astype(jnp.float32)
    hot = (jnp.transpose(codes) == q.astype(jnp.float32)).astype(jnp.float32).astype(jnp.bfloat16)
    for m in range(0, MODES, 2):
        pair = jnp.concatenate([plane(m), plane(m + 1)], axis=1)
        summed = jnp.dot(hot, pair, preferred_element_type=jnp.float32)
        wide[m * CODES : (m + 1) * CODES, :] = summed[:, :DOFS]
        wide[(m + 1) * CODES : (m + 2) * CODES, :] = summed[:, DOFS:]
    found = []
    for y in range(4):
        lefts, rights = [], []
        for j in range(ROWS_HERE):
            a0 = wide[pl.ds(y * 16 + j, MODES, stride=CODES), :]
            a1 = wide[pl.ds(64 + y * 16 + j, MODES, stride=CODES), :]
            lefts.append(jnp.concatenate([a0, a1], axis=0))
            side = jnp.broadcast_to(which[pl.ds(y * ROWS_HERE + j, 1), :], (MODES, DOFS))
            panel = panels[y, j].astype(jnp.float32)
            zero = jnp.zeros_like(panel)
            halves = [jnp.where(side == float(b), panel, zero) for b in range(AGG_DEV)]
            rights.append(jnp.concatenate(halves, axis=0).astype(jnp.bfloat16))
        left = jnp.concatenate(lefts, axis=1)
        high = left.astype(jnp.bfloat16)
        low = (left - high.astype(jnp.float32)).astype(jnp.bfloat16)
        right = jnp.concatenate(rights, axis=1)
        over = (((1,), (1,)), ((), ()))
        found.append(
            lax.dot_general(high, right, over, preferred_element_type=jnp.float32)
            + lax.dot_general(low, right, over, preferred_element_type=jnp.float32)
        )
    row = jnp.concatenate(found, axis=1)
    first = row[:, :128]
    rest = jnp.concatenate([row[:MODES, 128:], row[MODES:, 128:]], axis=1)
    for u in range(4):
        out[u, :PAIR, :] = first
        out[u, PAIR:, :] = rest


def place_kernel(parts, out, wide):
    yh, zl = lax.axis_index("yh"), lax.axis_index("zl")
    row = yh * 8 + lax.axis_index("zh") * 2 + zl
    lane = lax.broadcasted_iota(jnp.int32, (PAIR, 384), 1)
    wide[:, : 6 * 128] = jnp.zeros((PAIR, 6 * 128), jnp.float32)
    wide[:, 18 * 128 :] = jnp.zeros((PAIR, 7 * 128), jnp.float32)
    for ahead in range(4):
        block = jnp.zeros((PAIR, 384), jnp.float32)
        for low in range(2):
            part = parts[member(yh, ahead) * 2 + (low ^ zl)]
            rest = part[PAIR:, :]
            tail = jnp.concatenate([rest, pltpu.roll(rest, 64, axis=1)], axis=0)
            source = jnp.concatenate([part[:PAIR, :], tail, jnp.zeros_like(tail)], axis=1)
            for y in range(4):
                start = (y * 2 + low) * PAIR
                turned = pltpu.roll(source, (start - y * PAIR) % 384, axis=1)
                block = jnp.where((lane >= start) & (lane < start + PAIR), turned, block)
        at = (6 + 3 * ((yh + ahead) & 3)) * 128
        wide[:, pl.ds(pl.multiple_of(at, 128), 384)] = block
    offset = row * PAIR
    base = pl.multiple_of((offset // 128) * 128, 128)
    shift = offset % 128
    narrow = lax.broadcasted_iota(jnp.int32, (PAIR, 128), 1)
    turned = []
    for t in range(14):
        tile = wide[:, pl.ds(base + t * 128, 128)]
        turned.append(pltpu.roll(tile, (128 - shift) % 128, axis=1))
    for t in range(13):
        tile = jnp.where(narrow < 128 - shift, turned[t], turned[t + 1])
        width = min(128, WIN - t * 128)
        for a in range(AGG_DEV):
            out[a, :, t * 128 : t * 128 + width] = tile[a * MODES : (a + 1) * MODES, :width]


def everything(space, count):
    return [pl.BlockSpec(memory_space=space) for _ in range(count)]


VMEM, SMEM = pltpu.VMEM, pltpu.SMEM


def local(blocks, columns, counts, aggregate, panels):
    f32, bf16 = jnp.float32, jnp.bfloat16
    params = pltpu.CompilerParams(vmem_limit_bytes=LIMIT)

    pairs = []
    for yh, zh, zl, yl, xh, xl, k in np.ndindex(*SIZES):
        ahead = ahead_of(yh, yl, xl)
        other = 1 - yl if ahead else yl
        source = ((yh + ahead) & 3, zh, zl ^ k, other, xh, xl, k)
        target = (yh, zh, zl, yl, xh, xl, k)
        pairs.append(tuple(int(np.ravel_multi_index(at, SIZES)) for at in (source, target)))
    turned = lax.ppermute(panels, AXES, pairs)

    left = pl.pallas_call(
        left_kernel,
        out_shape=jax.ShapeDtypeStruct((PLANES * SLOTS, DOFS), bf16),
        in_specs=everything(pltpu.HBM, 5),
        out_specs=pl.BlockSpec(memory_space=VMEM),
        scratch_shapes=[
            pltpu.VMEM((PLANES * SLOTS, DOFS), f32),
            pltpu.VMEM(blocks.shape, bf16),
            pltpu.SMEM((2, ROWS_HERE), jnp.int32),
            pltpu.SMEM((1, ROWS_HERE), jnp.int32),
            pltpu.SMEM(aggregate.shape, jnp.int32),
            pltpu.VMEM(panels.shape, bf16),
            pltpu.SemaphoreType.DMA((9,)),
        ],
        compiler_params=pltpu.CompilerParams(vmem_limit_bytes=FULL),
        cost_estimate=pl.CostEstimate(flops=25_000_000, bytes_accessed=2_000_000, transcendentals=0),
        name="left",
    )(blocks, columns.T, counts.T, aggregate, panels)
    def flips(groups, *names):
        pairs = []
        for at in np.ndindex(*SIZES):
            if at[1] in groups:
                to = tuple(1 - c if n in names else c for n, c in zip(AXES, at))
                pairs.append((int(np.ravel_multi_index(at, SIZES)), int(np.ravel_multi_index(to, SIZES))))
        return pairs

    def swapped(x, groups, *names):
        return lax.ppermute(x, AXES, flips(groups, *names))

    first, last = range(EARLY), range(EARLY, SIZES[1])
    most, least = range(EARLY + 1), range(EARLY + 1, SIZES[1])

    which = pl.pallas_call(
        halves_kernel,
        out_shape=jax.ShapeDtypeStruct((4 * ROWS_HERE, DOFS), f32),
        in_specs=everything(pltpu.HBM, 1),
        out_specs=pl.BlockSpec(memory_space=VMEM),
        scratch_shapes=[pltpu.SMEM(aggregate.shape, jnp.int32), pltpu.SemaphoreType.DMA],
        compiler_params=params,
        cost_estimate=pl.CostEstimate(flops=100_000_000_000, bytes_accessed=1_000, transcendentals=0),
        name="halves",
    )(aggregate)
    across = swapped(left, most, "yl", "xl")
    early = [swapped(left, first, "xl"), swapped(left, first, "yl")]
    far_early = swapped(jnp.stack([left, *early, across]), first, "k")
    copies = pl.pallas_call(
        spread_kernel,
        out_shape=jax.ShapeDtypeStruct((4,) + turned.shape, bf16),
        in_specs=[pl.BlockSpec(memory_space=VMEM)],
        out_specs=pl.BlockSpec(memory_space=pl.ANY),
        scratch_shapes=[pltpu.SemaphoreType.DMA((4,))],
        compiler_params=params,
        cost_estimate=pl.CostEstimate(flops=100_000_000_000, bytes_accessed=500_000, transcendentals=0),
        name="copies",
    )(turned)
    gathered = lax.all_to_all(copies, "zh", 0, 0, tiled=True)
    left_later, far_early, which = lax.optimization_barrier((left, far_early, which))
    late = [swapped(left_later, last, "xl"), swapped(left_later, last, "yl")]
    late.append(swapped(left_later, least, "yl", "xl"))
    late, gathered = lax.optimization_barrier((late, gathered))
    near = jnp.stack([left, *(one + two for one, two in zip([*early, across], late))])
    far_late = swapped(near, last, "k")

    part = pl.pallas_call(
        middle_kernel,
        out_shape=jax.ShapeDtypeStruct((4, PAIR + MODES, DOFS), f32),
        in_specs=[
            pl.BlockSpec(memory_space=VMEM),
            pl.BlockSpec(memory_space=VMEM),
            pl.BlockSpec(memory_space=VMEM),
            pl.BlockSpec(memory_space=VMEM),
            pl.BlockSpec(memory_space=VMEM),
        ],
        out_specs=pl.BlockSpec(memory_space=VMEM),
        scratch_shapes=[pltpu.VMEM((MODES * CODES, DOFS), f32)],
        compiler_params=params,
        cost_estimate=pl.CostEstimate(flops=500_000_000, bytes_accessed=3_000_000, transcendentals=0),
        name="middle",
    )(near, far_early, far_late, gathered, which)

    shares = lax.all_to_all(part, "xh", 0, 0, tiled=True)
    whole = jnp.sum(shares, axis=0)
    spread = lax.all_to_all(
        jnp.broadcast_to(whole[None], (8,) + whole.shape), SHARE, 0, 0, tiled=True
    )
    return pl.pallas_call(
        place_kernel,
        out_shape=jax.ShapeDtypeStruct((AGG_DEV, MODES, WIN), f32),
        in_specs=[pl.BlockSpec(memory_space=VMEM)],
        out_specs=pl.BlockSpec(memory_space=VMEM),
        scratch_shapes=[pltpu.VMEM((PAIR, 25 * 128), f32)],
        compiler_params=params,
        cost_estimate=pl.CostEstimate(flops=1_000_000, bytes_accessed=600_000, transcendentals=0),
        name="place",
    )(spread)


def solution(mesh):
    inner = Mesh(mesh.devices.reshape(SIZES), AXES)
    return jax.shard_map(
        local,
        mesh=inner,
        in_specs=(
            P(ROWS, COLS, None, None),
            P(ROWS, COLS),
            P(ROWS, COLS),
            P(),
            P(ROWS, None, None),
        ),
        out_specs=P(ROWS, None, None),
        check_vma=False,
    )
```

```python
import functools

import jax
import jax.numpy as jnp
import numpy as np
from jax import lax
from jax.experimental import pallas as pl
from jax.experimental.pallas import tpu as pltpu
from jax.sharding import Mesh
from jax.sharding import PartitionSpec as P

AXES = ("yh", "zh", "zl", "yl", "xh", "xl", "k")
SIZES = (4, 4, 2, 2, 4, 2, 2)
ROWS = ("yh", "zh", "zl")
COLS = ("yl", "xh", "xl", "k")
SHARE = ("yl", "xl", "k")
QUAD = ("yl", "xl")

ROWS_HERE = 16
SLOTS = 32
MODES = 24
DOFS = 128
AGG_DEV = 2
PAIR = AGG_DEV * MODES
CODES = AGG_DEV * 4 * ROWS_HERE
EARLY = 2
PLANES = MODES + 1
WIN = 1584
LIMIT = 24 * 1024 * 1024
FULL = 63 * 1024 * 1024


def member(yh, ahead):
    odd = ahead & 1
    return odd * (4 - ahead) + (1 - odd) * 2 * ((ahead >> 1) ^ (yh >> 1))


def ahead_of(yh, yl, xl):
    return xl * (3 - 2 * yl) + (1 - xl) * 2 * (yl ^ (yh >> 1))


def left_kernel(*refs):
    far = refs[:5]
    out, wide, blocks, columns, counts, aggregate, panels, arrived = refs[5:]
    pieces = 4
    step = ROWS_HERE // pieces
    copies = [
        pltpu.make_async_copy(far[n], here, arrived.at[n])
        for n, here in ((1, columns), (2, counts), (3, aggregate), (4, panels))
    ]
    for p in range(pieces):
        part = pl.ds(p * step, step)
        copies.append(pltpu.make_async_copy(far[0].at[part], blocks.at[part], arrived.at[5 + p]))
    for copy in copies:
        copy.start()
    for copy in copies[:3]:
        copy.wait()
    row = lax.axis_index("yh") * 8 + lax.axis_index("zh") * 2 + lax.axis_index("zl")
    yh, zl = lax.axis_index("yh"), lax.axis_index("zl")
    lane = lax.broadcasted_iota(jnp.int32, (1, DOFS), 1)
    for i in range(ROWS_HERE):
        count = counts[0, i]
        own = aggregate[row * ROWS_HERE + i] - row * AGG_DEV
        for s in range(2):
            column = columns[s, i]
            code = own * 64 + ((column >> 5) & 3) * 16 + (column & 15)
            code = jnp.where(s < count, code, -1)
            place = member(yh, ((column >> 7) - yh) & 3) * 2 + (((column >> 4) & 1) ^ zl)
            at = MODES * SLOTS + 2 * i + s
            wide[pl.ds(at, 1), :] = jnp.where(lane == code, place, -1).astype(jnp.float32)
    copies[3].wait()
    for i in range(ROWS_HERE):
        if i % step == 0:
            copies[4 + i // step].wait()
        both = jnp.concatenate([blocks[i, 0], blocks[i, 1]], axis=1)
        left = jnp.dot(panels[i], both, preferred_element_type=jnp.float32)
        for s in range(2):
            wide[pl.ds(2 * i + s, MODES, stride=SLOTS), :] = left[:, s * DOFS : (s + 1) * DOFS]
    out[...] = wide[...].astype(jnp.bfloat16)


def spread_kernel(one, out, arrived):
    copies = [pltpu.make_async_copy(one, out.at[u], arrived.at[u]) for u in range(4)]
    for copy in copies:
        copy.start()
    for copy in copies:
        copy.wait()


def halves_kernel(aggregate_far, out, aggregate, arrived):
    copy = pltpu.make_async_copy(aggregate_far, aggregate, arrived)
    copy.start()
    copy.wait()
    yh = lax.axis_index("yh")
    high = (yh + ahead_of(yh, lax.axis_index("yl"), lax.axis_index("xl"))) & 3
    low = lax.axis_index("zl") ^ lax.axis_index("k")
    for y in range(4):
        group = high * 8 + y * 2 + low
        for j in range(ROWS_HERE):
            which = aggregate[group * ROWS_HERE + j] - group * AGG_DEV
            out[pl.ds(y * ROWS_HERE + j, 1), :] = jnp.full((1, DOFS), which, jnp.int32).astype(jnp.float32)


def middle_kernel(near, far, far_late, panels, which, out, wide):
    q = lax.axis_index("yl") * 4 + lax.axis_index("xl") * 2 + lax.axis_index("k")

    def plane(m):
        rows = slice(m * SLOTS, (m + 1) * SLOTS)
        parts = [near[u, rows, :] for u in range(4)] + [far[u, rows, :] + far_late[u, rows, :] for u in range(4)]
        return jnp.concatenate(parts, axis=0)

    codes = plane(MODES).astype(jnp.float32)
    hot = (jnp.transpose(codes) == q.astype(jnp.float32)).astype(jnp.float32).astype(jnp.bfloat16)
    for m in range(0, MODES, 2):
        pair = jnp.concatenate([plane(m), plane(m + 1)], axis=1)
        summed = jnp.dot(hot, pair, preferred_element_type=jnp.float32)
        wide[m * CODES : (m + 1) * CODES, :] = summed[:, :DOFS]
        wide[(m + 1) * CODES : (m + 2) * CODES, :] = summed[:, DOFS:]
    found = []
    for y in range(4):
        lefts, rights = [], []
        for j in range(ROWS_HERE):
            a0 = wide[pl.ds(y * 16 + j, MODES, stride=CODES), :]
            a1 = wide[pl.ds(64 + y * 16 + j, MODES, stride=CODES), :]
            lefts.append(jnp.concatenate([a0, a1], axis=0))
            side = jnp.broadcast_to(which[pl.ds(y * ROWS_HERE + j, 1), :], (MODES, DOFS))
            panel = panels[y, j].astype(jnp.float32)
            zero = jnp.zeros_like(panel)
            halves = [jnp.where(side == float(b), panel, zero) for b in range(AGG_DEV)]
            rights.append(jnp.concatenate(halves, axis=0).astype(jnp.bfloat16))
        left = jnp.concatenate(lefts, axis=1)
        high = left.astype(jnp.bfloat16)
        low = (left - high.astype(jnp.float32)).astype(jnp.bfloat16)
        right = jnp.concatenate(rights, axis=1)
        over = (((1,), (1,)), ((), ()))
        found.append(
            lax.dot_general(high, right, over, preferred_element_type=jnp.float32)
            + lax.dot_general(low, right, over, preferred_element_type=jnp.float32)
        )
    row = jnp.concatenate(found, axis=1)
    first = row[:, :128]
    rest = jnp.concatenate([row[:MODES, 128:], row[MODES:, 128:]], axis=1)
    for u in range(4):
        out[u, :PAIR, :] = first
        out[u, PAIR:, :] = rest


def place_kernel(parts, out, wide):
    yh, zl = lax.axis_index("yh"), lax.axis_index("zl")
    row = yh * 8 + lax.axis_index("zh") * 2 + zl
    lane = lax.broadcasted_iota(jnp.int32, (PAIR, 256), 1)
    wide[:, : 6 * 128] = jnp.zeros((PAIR, 6 * 128), jnp.float32)
    wide[:, 18 * 128 :] = jnp.zeros((PAIR, 7 * 128), jnp.float32)
    for ahead in range(4):
        windows = [jnp.zeros((PAIR, 256), jnp.float32) for _ in range(2)]
        for low in range(2):
            part = parts[member(yh, ahead) * 2 + (low ^ zl)]
            rest = part[PAIR:, :]
            tail = jnp.concatenate([rest, pltpu.roll(rest, 64, axis=1)], axis=0)
            source = jnp.concatenate([part[:PAIR, :], tail], axis=1)
            for y in range(4):
                start = (y * 2 + low) * PAIR
                w = 0 if start < 240 else 1
                at = start - 128 * w
                turned = pltpu.roll(source, (at - y * PAIR) % 256, axis=1)
                windows[w] = jnp.where((lane >= at) & (lane < at + PAIR), turned, windows[w])
        first, last = windows
        block = jnp.concatenate([first[:, :128], first[:, 128:] + last[:, :128], last[:, 128:]], axis=1)
        at = (6 + 3 * ((yh + ahead) & 3)) * 128
        wide[:, pl.ds(pl.multiple_of(at, 128), 384)] = block
    offset = row * PAIR
    base = pl.multiple_of((offset // 128) * 128, 128)
    shift = offset % 128
    narrow = lax.broadcasted_iota(jnp.int32, (PAIR, 128), 1)
    turned = []
    for t in range(14):
        tile = wide[:, pl.ds(base + t * 128, 128)]
        turned.append(pltpu.roll(tile, (128 - shift) % 128, axis=1))
    for t in range(13):
        tile = jnp.where(narrow < 128 - shift, turned[t], turned[t + 1])
        width = min(128, WIN - t * 128)
        for a in range(AGG_DEV):
            out[a, :, t * 128 : t * 128 + width] = tile[a * MODES : (a + 1) * MODES, :width]


def everything(space, count):
    return [pl.BlockSpec(memory_space=space) for _ in range(count)]


VMEM, SMEM = pltpu.VMEM, pltpu.SMEM


def local(blocks, columns, counts, aggregate, panels):
    f32, bf16 = jnp.float32, jnp.bfloat16
    params = pltpu.CompilerParams(vmem_limit_bytes=LIMIT)

    pairs = []
    for yh, zh, zl, yl, xh, xl, k in np.ndindex(*SIZES):
        ahead = ahead_of(yh, yl, xl)
        other = 1 - yl if ahead else yl
        source = ((yh + ahead) & 3, zh, zl ^ k, other, xh, xl, k)
        target = (yh, zh, zl, yl, xh, xl, k)
        pairs.append(tuple(int(np.ravel_multi_index(at, SIZES)) for at in (source, target)))
    turned = lax.ppermute(panels, AXES, pairs)

    left = pl.pallas_call(
        left_kernel,
        out_shape=jax.ShapeDtypeStruct((PLANES * SLOTS, DOFS), bf16),
        in_specs=everything(pltpu.HBM, 5),
        out_specs=pl.BlockSpec(memory_space=VMEM),
        scratch_shapes=[
            pltpu.VMEM((PLANES * SLOTS, DOFS), f32),
            pltpu.VMEM(blocks.shape, bf16),
            pltpu.SMEM((2, ROWS_HERE), jnp.int32),
            pltpu.SMEM((1, ROWS_HERE), jnp.int32),
            pltpu.SMEM(aggregate.shape, jnp.int32),
            pltpu.VMEM(panels.shape, bf16),
            pltpu.SemaphoreType.DMA((9,)),
        ],
        compiler_params=pltpu.CompilerParams(vmem_limit_bytes=FULL),
        cost_estimate=pl.CostEstimate(flops=25_000_000, bytes_accessed=2_000_000, transcendentals=0),
        name="left",
    )(blocks, columns.T, counts.T, aggregate, panels)
    def flips(groups, *names):
        pairs = []
        for at in np.ndindex(*SIZES):
            if at[1] in groups:
                to = tuple(1 - c if n in names else c for n, c in zip(AXES, at))
                pairs.append((int(np.ravel_multi_index(at, SIZES)), int(np.ravel_multi_index(to, SIZES))))
        return pairs

    def swapped(x, groups, *names):
        return lax.ppermute(x, AXES, flips(groups, *names))

    first, last = range(EARLY), range(EARLY, SIZES[1])
    most, least = range(EARLY + 1), range(EARLY + 1, SIZES[1])

    which = pl.pallas_call(
        halves_kernel,
        out_shape=jax.ShapeDtypeStruct((4 * ROWS_HERE, DOFS), f32),
        in_specs=everything(pltpu.HBM, 1),
        out_specs=pl.BlockSpec(memory_space=VMEM),
        scratch_shapes=[pltpu.SMEM(aggregate.shape, jnp.int32), pltpu.SemaphoreType.DMA],
        compiler_params=params,
        cost_estimate=pl.CostEstimate(flops=100_000_000_000, bytes_accessed=1_000, transcendentals=0),
        name="halves",
    )(aggregate)
    across = swapped(left, most, "yl", "xl")
    early = [swapped(left, first, "xl"), swapped(left, first, "yl")]
    far_early = swapped(jnp.stack([left, *early, across]), first, "k")
    copies = pl.pallas_call(
        spread_kernel,
        out_shape=jax.ShapeDtypeStruct((4,) + turned.shape, bf16),
        in_specs=[pl.BlockSpec(memory_space=VMEM)],
        out_specs=pl.BlockSpec(memory_space=pl.ANY),
        scratch_shapes=[pltpu.SemaphoreType.DMA((4,))],
        compiler_params=params,
        cost_estimate=pl.CostEstimate(flops=100_000_000_000, bytes_accessed=500_000, transcendentals=0),
        name="copies",
    )(turned)
    gathered = lax.all_to_all(copies, "zh", 0, 0, tiled=True)
    left_later, far_early, which = lax.optimization_barrier((left, far_early, which))
    late = [swapped(left_later, last, "xl"), swapped(left_later, last, "yl")]
    late.append(swapped(left_later, least, "yl", "xl"))
    late, gathered = lax.optimization_barrier((late, gathered))
    near = jnp.stack([left, *(one + two for one, two in zip([*early, across], late))])
    far_late = swapped(near, last, "k")

    part = pl.pallas_call(
        middle_kernel,
        out_shape=jax.ShapeDtypeStruct((4, PAIR + MODES, DOFS), f32),
        in_specs=[
            pl.BlockSpec(memory_space=VMEM),
            pl.BlockSpec(memory_space=VMEM),
            pl.BlockSpec(memory_space=VMEM),
            pl.BlockSpec(memory_space=VMEM),
            pl.BlockSpec(memory_space=VMEM),
        ],
        out_specs=pl.BlockSpec(memory_space=VMEM),
        scratch_shapes=[pltpu.VMEM((MODES * CODES, DOFS), f32)],
        compiler_params=params,
        cost_estimate=pl.CostEstimate(flops=500_000_000, bytes_accessed=3_000_000, transcendentals=0),
        name="middle",
    )(near, far_early, far_late, gathered, which)

    shares = lax.all_to_all(part, "xh", 0, 0, tiled=True)
    whole = jnp.sum(shares, axis=0)
    spread = lax.all_to_all(
        jnp.broadcast_to(whole[None], (8,) + whole.shape), SHARE, 0, 0, tiled=True
    )
    return pl.pallas_call(
        place_kernel,
        out_shape=jax.ShapeDtypeStruct((AGG_DEV, MODES, WIN), f32),
        in_specs=[pl.BlockSpec(memory_space=VMEM)],
        out_specs=pl.BlockSpec(memory_space=VMEM),
        scratch_shapes=[pltpu.VMEM((PAIR, 25 * 128), f32)],
        compiler_params=params,
        cost_estimate=pl.CostEstimate(flops=1_000_000, bytes_accessed=600_000, transcendentals=0),
        name="place",
    )(spread)


def solution(mesh):
    inner = Mesh(mesh.devices.reshape(SIZES), AXES)
    return jax.shard_map(
        local,
        mesh=inner,
        in_specs=(
            P(ROWS, COLS, None, None),
            P(ROWS, COLS),
            P(ROWS, COLS),
            P(),
            P(ROWS, None, None),
        ),
        out_specs=P(ROWS, None, None),
        check_vma=False,
    )
```

```python
import functools

import jax
import jax.numpy as jnp
import numpy as np
from jax import lax
from jax.experimental import pallas as pl
from jax.experimental.pallas import tpu as pltpu
from jax.sharding import Mesh
from jax.sharding import PartitionSpec as P

AXES = ("yh", "zh", "zl", "yl", "xh", "xl", "k")
SIZES = (4, 4, 2, 2, 4, 2, 2)
ROWS = ("yh", "zh", "zl")
COLS = ("yl", "xh", "xl", "k")
SHARE = ("yl", "xl", "k")
QUAD = ("yl", "xl")

ROWS_HERE = 16
SLOTS = 32
MODES = 24
DOFS = 128
AGG_DEV = 2
PAIR = AGG_DEV * MODES
CODES = AGG_DEV * 4 * ROWS_HERE
EARLY = 2
PLANES = MODES + 1
WIN = 1584
LIMIT = 24 * 1024 * 1024
FULL = 63 * 1024 * 1024


def member(yh, ahead):
    odd = ahead & 1
    return odd * (4 - ahead) + (1 - odd) * 2 * ((ahead >> 1) ^ (yh >> 1))


def ahead_of(yh, yl, xl):
    return xl * (3 - 2 * yl) + (1 - xl) * 2 * (yl ^ (yh >> 1))


def left_kernel(*refs):
    far = refs[:5]
    out, wide, blocks, columns, counts, aggregate, panels, arrived = refs[5:]
    pieces = 4
    step = ROWS_HERE // pieces
    copies = [
        pltpu.make_async_copy(far[n], here, arrived.at[n])
        for n, here in ((1, columns), (2, counts), (3, aggregate), (4, panels))
    ]
    for p in range(pieces):
        part = pl.ds(p * step, step)
        copies.append(pltpu.make_async_copy(far[0].at[part], blocks.at[part], arrived.at[5 + p]))
    for copy in copies:
        copy.start()
    for copy in copies[:3]:
        copy.wait()
    row = lax.axis_index("yh") * 8 + lax.axis_index("zh") * 2 + lax.axis_index("zl")
    yh, zl = lax.axis_index("yh"), lax.axis_index("zl")
    lane = lax.broadcasted_iota(jnp.int32, (1, DOFS), 1)
    for i in range(ROWS_HERE):
        count = counts[0, i]
        own = aggregate[row * ROWS_HERE + i] - row * AGG_DEV
        for s in range(2):
            column = columns[s, i]
            code = own * 64 + ((column >> 5) & 3) * 16 + (column & 15)
            code = jnp.where(s < count, code, -1)
            place = member(yh, ((column >> 7) - yh) & 3) * 2 + (((column >> 4) & 1) ^ zl)
            at = MODES * SLOTS + 2 * i + s
            wide[pl.ds(at, 1), :] = jnp.where(lane == code, place, -1).astype(jnp.float32)
    copies[3].wait()
    for i in range(ROWS_HERE):
        if i % step == 0:
            copies[4 + i // step].wait()
        both = jnp.concatenate([blocks[i, 0], blocks[i, 1]], axis=1)
        left = jnp.dot(panels[i], both, preferred_element_type=jnp.float32)
        for s in range(2):
            wide[pl.ds(2 * i + s, MODES, stride=SLOTS), :] = left[:, s * DOFS : (s + 1) * DOFS]
    out[...] = wide[...].astype(jnp.bfloat16)


def spread_kernel(one, out, arrived):
    copies = [pltpu.make_async_copy(one, out.at[u], arrived.at[u]) for u in range(4)]
    for copy in copies:
        copy.start()
    for copy in copies:
        copy.wait()


def halves_kernel(aggregate_far, out, aggregate, arrived):
    copy = pltpu.make_async_copy(aggregate_far, aggregate, arrived)
    copy.start()
    copy.wait()
    yh = lax.axis_index("yh")
    high = (yh + ahead_of(yh, lax.axis_index("yl"), lax.axis_index("xl"))) & 3
    low = lax.axis_index("zl") ^ lax.axis_index("k")
    for y in range(4):
        group = high * 8 + y * 2 + low
        for j in range(ROWS_HERE):
            which = aggregate[group * ROWS_HERE + j] - group * AGG_DEV
            out[pl.ds(y * ROWS_HERE + j, 1), :] = jnp.full((1, DOFS), which, jnp.int32).astype(jnp.float32)


def middle_kernel(near, far, far_late, panels, which, out, wide):
    q = lax.axis_index("yl") * 4 + lax.axis_index("xl") * 2 + lax.axis_index("k")

    def plane(m):
        rows = slice(m * SLOTS, (m + 1) * SLOTS)
        parts = [near[u, rows, :] for u in range(4)] + [far[u, rows, :] + far_late[u, rows, :] for u in range(4)]
        return jnp.concatenate(parts, axis=0)

    codes = plane(MODES).astype(jnp.float32)
    hot = (jnp.transpose(codes) == q.astype(jnp.float32)).astype(jnp.float32).astype(jnp.bfloat16)
    for m in range(0, MODES, 2):
        pair = jnp.concatenate([plane(m), plane(m + 1)], axis=1)
        summed = jnp.dot(hot, pair, preferred_element_type=jnp.float32)
        wide[m * CODES : (m + 1) * CODES, :] = summed[:, :DOFS]
        wide[(m + 1) * CODES : (m + 2) * CODES, :] = summed[:, DOFS:]
    found = []
    for y in range(4):
        lefts, rights = [], []
        for j in range(ROWS_HERE):
            a0 = wide[pl.ds(y * 16 + j, MODES, stride=CODES), :]
            a1 = wide[pl.ds(64 + y * 16 + j, MODES, stride=CODES), :]
            lefts.append(jnp.concatenate([a0, a1], axis=0))
            side = jnp.broadcast_to(which[pl.ds(y * ROWS_HERE + j, 1), :], (MODES, DOFS))
            panel = panels[y, j].astype(jnp.float32)
            zero = jnp.zeros_like(panel)
            halves = [jnp.where(side == float(b), panel, zero) for b in range(AGG_DEV)]
            rights.append(jnp.concatenate(halves, axis=0).astype(jnp.bfloat16))
        left = jnp.concatenate(lefts, axis=1)
        high = left.astype(jnp.bfloat16)
        low = (left - high.astype(jnp.float32)).astype(jnp.bfloat16)
        right = jnp.concatenate(rights, axis=1)
        over = (((1,), (1,)), ((), ()))
        found.append(
            lax.dot_general(high, right, over, preferred_element_type=jnp.float32)
            + lax.dot_general(low, right, over, preferred_element_type=jnp.float32)
        )
    row = jnp.concatenate(found, axis=1)
    first = row[:, :128]
    rest = jnp.concatenate([row[:MODES, 128:], row[MODES:, 128:]], axis=1)
    for u in range(4):
        out[u, :PAIR, :] = first
        out[u, PAIR:, :] = rest


def place_kernel(parts, out, wide, held, sent):
    yh, zl = lax.axis_index("yh"), lax.axis_index("zl")
    row = yh * 8 + lax.axis_index("zh") * 2 + zl
    lane = lax.broadcasted_iota(jnp.int32, (PAIR, 256), 1)
    wide[:, : 6 * 128] = jnp.zeros((PAIR, 6 * 128), jnp.float32)
    wide[:, 18 * 128 :] = jnp.zeros((PAIR, 7 * 128), jnp.float32)
    for ahead in range(4):
        windows = [jnp.zeros((PAIR, 256), jnp.float32) for _ in range(2)]
        for low in range(2):
            part = parts[member(yh, ahead) * 2 + (low ^ zl)]
            rest = part[PAIR:, :]
            tail = jnp.concatenate([rest, pltpu.roll(rest, 64, axis=1)], axis=0)
            source = jnp.concatenate([part[:PAIR, :], tail], axis=1)
            for y in range(4):
                start = (y * 2 + low) * PAIR
                w = 0 if start < 240 else 1
                at = start - 128 * w
                turned = pltpu.roll(source, (at - y * PAIR) % 256, axis=1)
                windows[w] = jnp.where((lane >= at) & (lane < at + PAIR), turned, windows[w])
        first, last = windows
        block = jnp.concatenate([first[:, :128], first[:, 128:] + last[:, :128], last[:, 128:]], axis=1)
        at = (6 + 3 * ((yh + ahead) & 3)) * 128
        wide[:, pl.ds(pl.multiple_of(at, 128), 384)] = block
    offset = row * PAIR
    base = pl.multiple_of((offset // 128) * 128, 128)
    shift = offset % 128
    narrow = lax.broadcasted_iota(jnp.int32, (MODES, 128), 1)
    copies = []
    for a in range(AGG_DEV):
        rows = slice(a * MODES, (a + 1) * MODES)
        turned = []
        for t in range(14):
            tile = wide[rows, pl.ds(base + t * 128, 128)]
            turned.append(pltpu.roll(tile, (128 - shift) % 128, axis=1))
        for t in range(13):
            tile = jnp.where(narrow < 128 - shift, turned[t], turned[t + 1])
            width = min(128, WIN - t * 128)
            held[a, :, t * 128 : t * 128 + width] = tile[:, :width]
        copies.append(pltpu.make_async_copy(held.at[a], out.at[a], sent.at[a]))
        copies[a].start()
    for copy in copies:
        copy.wait()


def everything(space, count):
    return [pl.BlockSpec(memory_space=space) for _ in range(count)]


VMEM, SMEM = pltpu.VMEM, pltpu.SMEM


def local(blocks, columns, counts, aggregate, panels):
    f32, bf16 = jnp.float32, jnp.bfloat16
    params = pltpu.CompilerParams(vmem_limit_bytes=LIMIT)

    pairs = []
    for yh, zh, zl, yl, xh, xl, k in np.ndindex(*SIZES):
        ahead = ahead_of(yh, yl, xl)
        other = 1 - yl if ahead else yl
        source = ((yh + ahead) & 3, zh, zl ^ k, other, xh, xl, k)
        target = (yh, zh, zl, yl, xh, xl, k)
        pairs.append(tuple(int(np.ravel_multi_index(at, SIZES)) for at in (source, target)))
    turned = lax.ppermute(panels, AXES, pairs)

    left = pl.pallas_call(
        left_kernel,
        out_shape=jax.ShapeDtypeStruct((PLANES * SLOTS, DOFS), bf16),
        in_specs=everything(pltpu.HBM, 5),
        out_specs=pl.BlockSpec(memory_space=VMEM),
        scratch_shapes=[
            pltpu.VMEM((PLANES * SLOTS, DOFS), f32),
            pltpu.VMEM(blocks.shape, bf16),
            pltpu.SMEM((2, ROWS_HERE), jnp.int32),
            pltpu.SMEM((1, ROWS_HERE), jnp.int32),
            pltpu.SMEM(aggregate.shape, jnp.int32),
            pltpu.VMEM(panels.shape, bf16),
            pltpu.SemaphoreType.DMA((9,)),
        ],
        compiler_params=pltpu.CompilerParams(vmem_limit_bytes=FULL),
        cost_estimate=pl.CostEstimate(flops=25_000_000, bytes_accessed=2_000_000, transcendentals=0),
        name="left",
    )(blocks, columns.T, counts.T, aggregate, panels)
    def flips(groups, *names):
        pairs = []
        for at in np.ndindex(*SIZES):
            if at[1] in groups:
                to = tuple(1 - c if n in names else c for n, c in zip(AXES, at))
                pairs.append((int(np.ravel_multi_index(at, SIZES)), int(np.ravel_multi_index(to, SIZES))))
        return pairs

    def swapped(x, groups, *names):
        return lax.ppermute(x, AXES, flips(groups, *names))

    first, last = range(EARLY), range(EARLY, SIZES[1])
    most, least = range(EARLY + 1), range(EARLY + 1, SIZES[1])

    which = pl.pallas_call(
        halves_kernel,
        out_shape=jax.ShapeDtypeStruct((4 * ROWS_HERE, DOFS), f32),
        in_specs=everything(pltpu.HBM, 1),
        out_specs=pl.BlockSpec(memory_space=VMEM),
        scratch_shapes=[pltpu.SMEM(aggregate.shape, jnp.int32), pltpu.SemaphoreType.DMA],
        compiler_params=params,
        cost_estimate=pl.CostEstimate(flops=100_000_000_000, bytes_accessed=1_000, transcendentals=0),
        name="halves",
    )(aggregate)
    across = swapped(left, most, "yl", "xl")
    early = [swapped(left, first, "xl"), swapped(left, first, "yl")]
    far_early = swapped(jnp.stack([left, *early, across]), first, "k")
    copies = pl.pallas_call(
        spread_kernel,
        out_shape=jax.ShapeDtypeStruct((4,) + turned.shape, bf16),
        in_specs=[pl.BlockSpec(memory_space=VMEM)],
        out_specs=pl.BlockSpec(memory_space=pl.ANY),
        scratch_shapes=[pltpu.SemaphoreType.DMA((4,))],
        compiler_params=params,
        cost_estimate=pl.CostEstimate(flops=100_000_000_000, bytes_accessed=500_000, transcendentals=0),
        name="copies",
    )(turned)
    gathered = lax.all_to_all(copies, "zh", 0, 0, tiled=True)
    left_later, far_early, which = lax.optimization_barrier((left, far_early, which))
    late = [swapped(left_later, last, "xl"), swapped(left_later, last, "yl")]
    late.append(swapped(left_later, least, "yl", "xl"))
    late, gathered = lax.optimization_barrier((late, gathered))
    near = jnp.stack([left, *(one + two for one, two in zip([*early, across], late))])
    far_late = swapped(near, last, "k")

    part = pl.pallas_call(
        middle_kernel,
        out_shape=jax.ShapeDtypeStruct((4, PAIR + MODES, DOFS), f32),
        in_specs=[
            pl.BlockSpec(memory_space=VMEM),
            pl.BlockSpec(memory_space=VMEM),
            pl.BlockSpec(memory_space=VMEM),
            pl.BlockSpec(memory_space=VMEM),
            pl.BlockSpec(memory_space=VMEM),
        ],
        out_specs=pl.BlockSpec(memory_space=VMEM),
        scratch_shapes=[pltpu.VMEM((MODES * CODES, DOFS), f32)],
        compiler_params=params,
        cost_estimate=pl.CostEstimate(flops=500_000_000, bytes_accessed=3_000_000, transcendentals=0),
        name="middle",
    )(near, far_early, far_late, gathered, which)

    shares = lax.all_to_all(part, "xh", 0, 0, tiled=True)
    whole = jnp.sum(shares, axis=0)
    spread = lax.all_to_all(
        jnp.broadcast_to(whole[None], (8,) + whole.shape), SHARE, 0, 0, tiled=True
    )
    return pl.pallas_call(
        place_kernel,
        out_shape=jax.ShapeDtypeStruct((AGG_DEV, MODES, WIN), f32),
        in_specs=[pl.BlockSpec(memory_space=VMEM)],
        out_specs=pl.BlockSpec(memory_space=pl.ANY),
        scratch_shapes=[
            pltpu.VMEM((PAIR, 25 * 128), f32),
            pltpu.VMEM((AGG_DEV, MODES, WIN), f32),
            pltpu.SemaphoreType.DMA((AGG_DEV,)),
        ],
        compiler_params=params,
        cost_estimate=pl.CostEstimate(flops=1_000_000, bytes_accessed=600_000, transcendentals=0),
        name="place",
    )(spread)


def solution(mesh):
    inner = Mesh(mesh.devices.reshape(SIZES), AXES)
    return jax.shard_map(
        local,
        mesh=inner,
        in_specs=(
            P(ROWS, COLS, None, None),
            P(ROWS, COLS),
            P(ROWS, COLS),
            P(),
            P(ROWS, None, None),
        ),
        out_specs=P(ROWS, None, None),
        check_vma=False,
    )
```
